32 devices in a mesh: pairs: 8 (over y, x, core), coef: 4 (over z).
Axes of the slice: x: 2, y: 2, z: 4, core: 2. Of those that a mesh axis runs over, the one named last changes fastest.
Arguments:
- integrals: bfloat16 [4096, 32, 64, 64], P('pairs', 'coef'), may hold values from -6 to 6
- block_shells: int32 [8, 32, 2], P('pairs', 'coef'), may hold values from 0 to 143
- live_counts: int32 [8, 4], P('pairs', 'coef'), may hold values from 1 to 8, as said below
- significance: int32 [144, 144], replicated, may hold values 0 or 1
- occ_coef: bfloat16 [9216, 64], P('coef'), may hold values from -0.375 to 0.375
- lam_coef: bfloat16 [64, 128], P('coef'), may hold values from -0.75 to 0.75
- sig_coef: bfloat16 [64, 128], P('coef'), may hold values from -0.75 to 0.75
Outputs:
- mo_integrals: float32 [4096, 128, 128], P(('pairs', 'coef'))
The draws below stay inside these ranges and needn't reach their ends.
Inputs may be any that keep to these rules, and one draw needn't show every extreme that they name: `live_counts`: each device's live slots are its first ones; some device has all 8 live.
All inputs are finite; a program needn't handle non-finite values.
Results may differ from the reference program's by a relative error of at most 0.0029.
Values may be sent and summed in bfloat16 or wider, within the bound.
A program may use at most 128 MiB of HBM per device.

```python
import jax
import jax.numpy as jnp
from jax import lax

SHELL = 64
NSH = 144
OCC = 64
LAMW = 64
SIGW = 64
VIRT = 128
NBLK = 8
NBF = 9216
LS = 4096
N_PAIRS = 8
N_COEF = 4


def draw_live_counts(key, part):
    key = jax.random.fold_in(key, 11)
    first_key, second_key = jax.random.split(key)
    total = N_PAIRS * N_COEF
    values = jax.random.randint(first_key, (total,), 1, NBLK + 1)
    chosen = jax.random.randint(second_key, (), 0, total)
    values = jnp.where(jnp.arange(total) == chosen, NBLK, values)
    return values.reshape(N_PAIRS, N_COEF).astype(jnp.int32)


def with_ends(drawn, stream_key, least, top_value):
    dims = drawn.shape
    spot = [jax.random.randint(jax.random.fold_in(stream_key, axis), (), 0, dims[axis]) for axis in range(len(dims))]
    drawn = drawn.at[tuple(spot)].set(least)
    longest = dims.index(max(dims))
    spot[longest] = (spot[longest] + 1) % dims[longest]
    return drawn.at[tuple(spot)].set(top_value)


def levels(rng, shape, pieces, smallest, top_value):
    def one(dim, blocks):
        steps = jax.random.uniform(jax.random.fold_in(jax.random.fold_in(rng, 6), dim), (blocks,), jnp.float32, smallest / len(pieces), top_value / len(pieces))
        return jnp.repeat(jnp.exp(steps), shape[dim] // blocks).reshape((-1,) + (1,) * (len(shape) - dim - 1))

    factor_of = one(*pieces[0])
    for cut in pieces[1:]:
        factor_of = factor_of * one(*cut)
    return factor_of


def centred(rng, shape, scale, bound, cuts=(), kind=jnp.bfloat16):
    loudness = levels(rng, shape, cuts, -0.22, 0.18) if cuts else 1.0
    entries = jax.random.normal(rng, shape, jnp.float32) * scale * loudness
    return jnp.minimum(jnp.maximum(entries, -bound), bound).astype(kind)


def setup_inputs(seed: int = 0) -> dict:
    key_list = jax.random.split(jax.random.key(seed), 8)
    integrals = centred(key_list[0], (LS, NBLK * N_COEF, SHELL, SHELL), 1.0, 6.0, ((0, 8), (1, 4)))
    block_shells = with_ends(jax.random.randint(key_list[1], (N_PAIRS, NBLK * N_COEF, 2), 0, NSH), jax.random.fold_in(key_list[1], 1), 0, NSH - 1).astype(jnp.int32)
    live_counts = draw_live_counts(jax.random.fold_in(key_list[7], 71), 0)
    significance = with_ends((jax.random.randint(key_list[3], (NSH, NSH), 0, 4) < 3).astype(jnp.int32), jax.random.fold_in(key_list[3], 1), 0, 1)
    occ_coef = centred(key_list[4], (NBF, OCC), 256 ** -0.5, 0.375, ((0, 4),))
    lam_coef = centred(key_list[5], (LAMW, VIRT), LAMW ** -0.5, 0.75, ((0, 4),))
    sig_coef = centred(key_list[6], (SIGW, VIRT), SIGW ** -0.5, 0.75, ((0, 4),))
    return {"integrals": integrals, "block_shells": block_shells, "live_counts": live_counts, "significance": significance, "occ_coef": occ_coef, "lam_coef": lam_coef, "sig_coef": sig_coef}


def reference(integrals, block_shells, live_counts, significance, occ_coef, lam_coef, sig_coef):
    slots_all = integrals.shape[1]
    per_device = slots_all // N_COEF
    shell_table = occ_coef.reshape(NSH, SHELL, OCC)
    grouped = integrals.reshape(N_PAIRS, LS // N_PAIRS, slots_all, SHELL, SHELL)

    def one_group(packed):
        tiles, shells_here, counts_here = packed
        rows = shell_table[shells_here[:, 0]].astype(jnp.float32)
        cols = shell_table[shells_here[:, 1]].astype(jnp.float32)
        screened = significance[shells_here[:, 0], shells_here[:, 1]]
        slot = jnp.arange(slots_all, dtype=jnp.int32)
        limit = counts_here[slot // per_device]
        live = ((slot % per_device) < limit) & (screened == 1)
        quarter = jnp.einsum("smi,lsmn->lsin", rows, tiles.astype(jnp.float32)).astype(jnp.bfloat16)
        weighted = cols * live.astype(jnp.float32)[:, None, None]
        return jnp.einsum("lsin,snj->lij", quarter.astype(jnp.float32), weighted)

    halves = lax.map(one_group, (grouped, block_shells, live_counts))
    pair_tensor = halves.reshape(LAMW, SIGW, OCC * OCC)
    partly = jnp.einsum("xa,xyq->qay", lam_coef.astype(jnp.float32), pair_tensor, precision=lax.Precision.HIGHEST)
    return jnp.einsum("qay,yb->qab", partly, sig_coef.astype(jnp.float32), precision=lax.Precision.HIGHEST)
```

```python
import functools

import jax
import jax.numpy as jnp
from jax import lax
from jax.experimental import pallas as pl
from jax.experimental.pallas import tpu as pltpu
from jax.sharding import PartitionSpec as P

LANES = 256
SUB = 4


def spread(block, inner, outer, first, second):
    a, b = block.shape
    rows = lax.broadcasted_iota(jnp.int32, (outer, a), 0)
    cols = lax.broadcasted_iota(jnp.int32, (outer, a), 1)
    pick_a = (first(rows) == cols).astype(jnp.bfloat16)
    rows = lax.broadcasted_iota(jnp.int32, (b, inner), 0)
    cols = lax.broadcasted_iota(jnp.int32, (b, inner), 1)
    pick_b = (second(cols) == rows).astype(jnp.bfloat16)
    left = jnp.dot(pick_a, block, preferred_element_type=jnp.float32).astype(jnp.bfloat16)
    return jnp.dot(left, pick_b, preferred_element_type=jnp.float32)


def half_kernel(row_ref, col_ref, tiles_ref, out_ref, lhs1, lhs2, wide, quarter):
    tile, slot = pl.program_id(0), pl.program_id(1)
    slots = pl.num_programs(1)
    shell = tiles_ref.shape[1]
    occ = row_ref.shape[1]
    k1 = SUB * shell
    n1 = SUB * occ
    k2 = SUB * shell
    n2 = SUB * occ

    @pl.when(tile == 0)
    def _():
        body = spread(row_ref[0], k1, n1, lambda r: r // SUB, lambda c: c % shell)
        r = lax.broadcasted_iota(jnp.int32, (n1, k1), 0)
        c = lax.broadcasted_iota(jnp.int32, (n1, k1), 1)
        lhs1[slot] = jnp.where(r % SUB == c // shell, body, 0.0).astype(jnp.bfloat16)
        body = spread(
            col_ref[0], k2, n2, lambda r: r % occ,
            lambda c: c // (SUB * SUB) * SUB + c % SUB,
        )
        r = lax.broadcasted_iota(jnp.int32, (n2, k2), 0)
        c = lax.broadcasted_iota(jnp.int32, (n2, k2), 1)
        lhs2[slot] = jnp.where(r // occ == c // SUB % SUB, body, 0.0).astype(jnp.bfloat16)

    wide[...] = tiles_ref[0].astype(jnp.float32)
    coef = lhs1[slot]
    step = SUB * SUB
    for q in range(shell // SUB):
        packed = jnp.concatenate(
            [wide[:, q * SUB + n, :].astype(jnp.bfloat16) for n in range(SUB)], axis=0
        )
        got = jnp.dot(coef, packed, preferred_element_type=jnp.float32).astype(jnp.bfloat16)
        quarter[slot, :, q * step:(q + 1) * step, :] = got.reshape(occ // SUB, step, got.shape[1])

    @pl.when(slot == slots - 1)
    def _():
        def one(iq, _):
            total = jnp.zeros((n2, out_ref.shape[1]), jnp.float32)
            for s in range(quarter.shape[0]):
                total = total + jnp.dot(lhs2[s], quarter[s, iq], preferred_element_type=jnp.float32)
            out_ref[pl.ds(pl.multiple_of(iq * n2, n2), n2), :] = total.astype(out_ref.dtype)
            return 0

        lax.fori_loop(0, occ // SUB, one, 0)


def half_sums(row_t, col_t, tiles):
    slots, shell, _, pairs = tiles.shape
    occ = row_t.shape[1]
    lanes = min(LANES, pairs)
    k = SUB * shell
    return pl.pallas_call(
        half_kernel,
        grid=(pairs // lanes, slots),
        out_shape=jax.ShapeDtypeStruct((occ * occ, pairs), jnp.bfloat16),
        in_specs=[
            pl.BlockSpec((1, occ, shell), lambda t, s: (s, 0, 0)),
            pl.BlockSpec((1, occ, shell), lambda t, s: (s, 0, 0)),
            pl.BlockSpec((1, shell, shell, lanes), lambda t, s: (s, 0, 0, t)),
        ],
        out_specs=pl.BlockSpec((occ * occ, lanes), lambda t, s: (0, t)),
        scratch_shapes=[
            pltpu.VMEM((slots, SUB * occ, k), jnp.bfloat16),
            pltpu.VMEM((slots, SUB * occ, k), jnp.bfloat16),
            pltpu.VMEM((shell, shell, lanes), jnp.float32),
            pltpu.VMEM((slots, occ // SUB, k, lanes), jnp.bfloat16),
        ],
        compiler_params=pltpu.CompilerParams(vmem_limit_bytes=48 * 2**20),
        name="half_sums",
    )(row_t, col_t, tiles)


def on_device(integrals, block_shells, live_counts, significance, occ_coef, lam_coef, sig_coef):
    occupied = lax.all_gather(occ_coef, "coef", axis=0, tiled=True)
    lam_panel = lax.all_gather(lam_coef, "coef", axis=0, tiled=True)
    sig_panel = lax.all_gather(sig_coef, "coef", axis=0, tiled=True)
    shell = integrals.shape[2]
    slots = integrals.shape[1]
    pairs = integrals.shape[0]
    occ = occupied.shape[1]
    table = occupied.reshape(-1, shell, occ)
    pair_shells = block_shells[0]
    rows = table[pair_shells[:, 0]]
    cols = table[pair_shells[:, 1]]
    screened = significance[pair_shells[:, 0], pair_shells[:, 1]]
    is_live = (jnp.arange(slots) < live_counts[0, 0]) & (screened == 1)
    cols = cols * is_live.astype(jnp.bfloat16)[:, None, None]
    half = half_sums(
        jnp.swapaxes(rows, 1, 2), jnp.swapaxes(cols, 1, 2), jnp.transpose(integrals, (1, 2, 3, 0))
    )
    n_pairs, n_coef = lax.axis_size("pairs"), lax.axis_size("coef")
    owners = n_pairs * n_coef
    owned_rows = occ * occ // owners
    moved = lax.all_to_all(
        half.reshape(owners, owned_rows, pairs), ("pairs", "coef"), split_axis=0, concat_axis=0, tiled=True
    )
    moved = moved.reshape(n_pairs, n_coef, owned_rows, pairs).astype(jnp.float32)
    owned = jnp.sum(moved, axis=1)
    lam_width, sig_width = lam_panel.shape[0], sig_panel.shape[0]
    grid = jnp.transpose(owned, (1, 0, 2)).reshape(owned_rows, lam_width, sig_width)
    partly = jnp.einsum(
        "xa,qxy->qay", lam_panel.astype(jnp.float32), grid, precision=lax.Precision.HIGHEST
    )
    return jnp.einsum(
        "qay,yb->qab", partly, sig_panel.astype(jnp.float32), precision=lax.Precision.HIGHEST
    )


def solution(mesh):
    placed = (
        P("pairs", "coef", None, None),
        P("pairs", "coef", None),
        P("pairs", "coef"),
        P(),
        P("coef", None),
        P("coef", None),
        P("coef", None),
    )
    return jax.shard_map(
        on_device,
        mesh=mesh,
        in_specs=placed,
        out_specs=P(("pairs", "coef"), None, None),
        check_vma=False,
    )
```

```python
import functools

import jax
import jax.numpy as jnp
from jax import lax
from jax.experimental import pallas as pl
from jax.experimental.pallas import tpu as pltpu
from jax.sharding import PartitionSpec as P

LANES = 256
SUB = 4


def spread(block, inner, outer, first, second):
    a, b = block.shape
    rows = lax.broadcasted_iota(jnp.int32, (outer, a), 0)
    cols = lax.broadcasted_iota(jnp.int32, (outer, a), 1)
    pick_a = (first(rows) == cols).astype(jnp.bfloat16)
    rows = lax.broadcasted_iota(jnp.int32, (b, inner), 0)
    cols = lax.broadcasted_iota(jnp.int32, (b, inner), 1)
    pick_b = (second(cols) == rows).astype(jnp.bfloat16)
    left = jnp.dot(pick_a, block, preferred_element_type=jnp.float32).astype(jnp.bfloat16)
    return jnp.dot(left, pick_b, preferred_element_type=jnp.float32)


def half_kernel(row_ref, col_ref, tiles_ref, out_ref, lhs2, wide, quarter):
    slot = pl.program_id(0)
    slots = pl.num_programs(0)
    shell = tiles_ref.shape[1]
    occ = row_ref.shape[1]
    k1 = SUB * shell
    n1 = SUB * occ
    k2 = SUB * shell
    n2 = SUB * occ

    body = spread(row_ref[0], k1, n1, lambda r: r // SUB, lambda c: c % shell)
    r = lax.broadcasted_iota(jnp.int32, (n1, k1), 0)
    c = lax.broadcasted_iota(jnp.int32, (n1, k1), 1)
    coef = jnp.where(r % SUB == c // shell, body, 0.0).astype(jnp.bfloat16)
    body = spread(
        col_ref[0], k2, n2, lambda r: r % occ,
        lambda c: c // (SUB * SUB) * SUB + c % SUB,
    )
    r = lax.broadcasted_iota(jnp.int32, (n2, k2), 0)
    c = lax.broadcasted_iota(jnp.int32, (n2, k2), 1)
    lhs2[slot] = jnp.where(r // occ == c // SUB % SUB, body, 0.0).astype(jnp.bfloat16)

    lanes = tiles_ref.shape[3]
    for h in range(lanes // 128):
        part = tiles_ref[0, :, :, h * 128:(h + 1) * 128].astype(jnp.float32)
        wide[h] = part.reshape(shell * shell, 128)
    step = SUB * SUB
    for q in range(shell // SUB):
        packed = jnp.concatenate(
            [
                jnp.concatenate(
                    [
                        wide[h, pl.ds(q * SUB + n, shell, stride=shell), :].astype(jnp.bfloat16)
                        for h in range(lanes // 128)
                    ],
                    axis=1,
                )
                for n in range(SUB)
            ],
            axis=0,
        )
        got = jnp.dot(coef, packed, preferred_element_type=jnp.float32).astype(jnp.bfloat16)
        quarter[slot, :, q * step:(q + 1) * step, :] = got.reshape(occ // SUB, step, got.shape[1])

    @pl.when(slot == slots - 1)
    def _():
        def one(iq, _):
            total = jnp.zeros((n2, out_ref.shape[1]), jnp.float32)
            for s in range(quarter.shape[0]):
                total = total + jnp.dot(lhs2[s], quarter[s, iq], preferred_element_type=jnp.float32)
            out_ref[pl.ds(pl.multiple_of(iq * n2, n2), n2), :] = total.astype(out_ref.dtype)
            return 0

        lax.fori_loop(0, occ // SUB, one, 0)


def half_sums(row_t, col_t, tiles, chunk, lanes):
    slots, shell, _, pairs = tiles.shape
    occ = row_t.shape[1]
    k = SUB * shell
    return pl.pallas_call(
        half_kernel,
        grid=(slots,),
        out_shape=jax.ShapeDtypeStruct((occ * occ, lanes), jnp.bfloat16),
        in_specs=[
            pl.BlockSpec((1, occ, shell), lambda s: (s, 0, 0)),
            pl.BlockSpec((1, occ, shell), lambda s: (s, 0, 0)),
            pl.BlockSpec((1, shell, shell, lanes), lambda s: (s, 0, 0, chunk)),
        ],
        out_specs=pl.BlockSpec((occ * occ, lanes), lambda s: (0, 0)),
        scratch_shapes=[
            pltpu.VMEM((slots, SUB * occ, k), jnp.bfloat16),
            pltpu.VMEM((lanes // 128, shell * shell, 128), jnp.float32),
            pltpu.VMEM((slots, occ // SUB, k, lanes), jnp.bfloat16),
        ],
        compiler_params=pltpu.CompilerParams(vmem_limit_bytes=40 * 2**20),
        cost_estimate=pl.CostEstimate(
            flops=2 * slots * shell * lanes * SUB * (shell * occ + occ * occ),
            bytes_accessed=2 * slots * shell * shell * lanes + 2 * occ * occ * lanes,
            transcendentals=0,
        ),
        name="half_sums",
    )(row_t, col_t, tiles)


def parts_of(x):
    high = x.astype(jnp.bfloat16)
    rest = x - high.astype(jnp.float32)
    mid = rest.astype(jnp.bfloat16)
    return high, mid, (rest - mid.astype(jnp.float32)).astype(jnp.bfloat16)


def virtual_kernel(chunks, *refs):
    moved, (lam_ref, sig_ref, out_ref, turned) = refs[:chunks], refs[chunks:]
    n_pairs, n_coef, rows, lanes = moved[0].shape
    virt = out_ref.shape[2]
    inner = sig_ref.shape[1] // virt
    for k, ref in enumerate(moved):
        total = ref[:, 0].astype(jnp.float32)
        for c in range(1, n_coef):
            total = total + ref[:, c].astype(jnp.float32)
        flat = total.reshape(n_pairs * rows, lanes)
        got = jnp.zeros((n_pairs * rows, inner * virt), jnp.float32)
        for part in reversed(parts_of(flat)):
            got = got + jnp.dot(part, sig_ref[...], preferred_element_type=jnp.float32)
        for x in range(inner):
            turned[k * inner + x] = got[:, x * virt:(x + 1) * virt]
    for q in range(rows):
        body = jnp.concatenate(
            [turned[x, pl.ds(q, n_pairs, stride=rows), :] for x in range(chunks * inner)], axis=0
        )
        out_ref[q] = jnp.dot(
            lam_ref[...], jnp.concatenate(parts_of(body), axis=0), preferred_element_type=jnp.float32
        )


def virtual(moved, lam_panel, sig_panel):
    n_pairs, n_coef, owned_rows, lanes = moved[0].shape
    lam_width, virt = lam_panel.shape
    sig_width = sig_panel.shape[0]
    inner = lanes // sig_width
    outer = len(moved) * inner
    rows = 16
    eye = jnp.eye(inner, dtype=jnp.bfloat16)
    sig_wide = (eye[:, None, :, None] * sig_panel[None, :, None, :]).reshape(lanes, inner * virt)
    lam_turned = lam_panel.reshape(n_pairs, outer, virt).transpose(2, 1, 0).reshape(virt, lam_width)
    lam_wide = jnp.concatenate([lam_turned] * 3, axis=1)
    return pl.pallas_call(
        functools.partial(virtual_kernel, len(moved)),
        grid=(owned_rows // rows,),
        out_shape=jax.ShapeDtypeStruct((owned_rows, virt, virt), jnp.float32),
        in_specs=[pl.BlockSpec((n_pairs, n_coef, rows, lanes), lambda t: (0, 0, t, 0)) for _ in moved]
        + [
            pl.BlockSpec(lam_wide.shape, lambda t: (0, 0)),
            pl.BlockSpec(sig_wide.shape, lambda t: (0, 0)),
        ],
        out_specs=pl.BlockSpec((rows, virt, virt), lambda t: (t, 0, 0)),
        scratch_shapes=[pltpu.VMEM((outer, n_pairs * rows, virt), jnp.float32)],
        compiler_params=pltpu.CompilerParams(vmem_limit_bytes=32 * 2**20),
        name="virtual",
    )(*moved, lam_wide, sig_wide)


def on_device(integrals, block_shells, live_counts, significance, occ_coef, lam_coef, sig_coef):
    occupied = lax.all_gather(occ_coef, "coef", axis=0, tiled=True)
    virt = lam_coef.shape[1]
    both = jnp.concatenate([lam_coef, sig_coef], axis=1)
    both = lax.all_gather(both, "coef", axis=0, tiled=True)
    occupied, both = lax.optimization_barrier((occupied, both))
    lam_panel, sig_panel = both[:, :virt], both[:, virt:]
    shell = integrals.shape[2]
    slots = integrals.shape[1]
    pairs = integrals.shape[0]
    occ = occupied.shape[1]
    table = occupied.reshape(-1, shell, occ)
    pair_shells = block_shells[0]
    rows = table[pair_shells[:, 0]]
    cols = table[pair_shells[:, 1]]
    screened = significance[pair_shells[:, 0], pair_shells[:, 1]]
    is_live = (jnp.arange(slots) < live_counts[0, 0]) & (screened == 1)
    cols = cols * is_live.astype(jnp.bfloat16)[:, None, None]
    row_t, col_t = jnp.swapaxes(rows, 1, 2), jnp.swapaxes(cols, 1, 2)
    tiles = jnp.transpose(integrals, (1, 2, 3, 0))
    n_pairs, n_coef = lax.axis_size("pairs"), lax.axis_size("coef")
    owners = n_pairs * n_coef
    owned_rows = occ * occ // owners
    lanes = min(LANES, pairs)
    sums = []
    for chunk in range(pairs // lanes):
        half = half_sums(row_t, col_t, tiles, chunk, lanes)
        moved = lax.all_to_all(
            half.reshape(owners, owned_rows, lanes), ("pairs", "coef"), split_axis=0, concat_axis=0, tiled=True
        )
        sums.append(moved.reshape(n_pairs, n_coef, owned_rows, lanes))
    return virtual(sums, lam_panel, sig_panel)


def solution(mesh):
    placed = (
        P("pairs", "coef", None, None),
        P("pairs", "coef", None),
        P("pairs", "coef"),
        P(),
        P("coef", None),
        P("coef", None),
        P("coef", None),
    )
    return jax.shard_map(
        on_device,
        mesh=mesh,
        in_specs=placed,
        out_specs=P(("pairs", "coef"), None, None),
        check_vma=False,
    )
```
